32 devices in a mesh: seg: 32 (over z, y, x, core).
Axes of the slice: x: 2, y: 2, z: 4, core: 2. Of those that a mesh axis runs over, the one named last changes fastest.
Arguments:
- density: float32 [2, 12288, 256], P(None, 'seg'), may hold values from -6 to 6
- near_blocks: bfloat16 [3, 2, 12288, 384], P(None, None, 'seg'), may hold values from -0.21875 to 0.21875
- projection: bfloat16 [2, 6144, 384], P(None, 'seg'), may hold values from -0.21875 to 0.21875
- transfers: bfloat16 [5, 2, 6144, 192], P(None, None, 'seg'), may hold values from -0.3125 to 0.3125
- interpolation: bfloat16 [2, 12288, 192], P(None, 'seg'), may hold values from -0.3125 to 0.3125
- precondition: float32 [2, 12288], P(None, 'seg'), may hold values from 0.5 to 1.5
Outputs:
- result: float32 [2, 12288, 256], P(None, 'seg')
The draws below stay inside these ranges and needn't reach their ends.
All inputs are finite; a program needn't handle non-finite values.
Results may differ from the reference program's by a relative error of at most 0.007.
Values may be sent and summed in bfloat16 or wider, within the bound.
A program may use at most 64 MiB of HBM per device.

```python
import jax
import jax.numpy as jnp
from jax import lax

C = 384
R = 192
ANG = 256
LEVELS = 5
SEGS = 32


def levels(stream_key, shape, shards, least, high):
    level = 1.0
    for axis_at, blocks in shards:
        steps = jax.random.uniform(jax.random.fold_in(jax.random.fold_in(stream_key, 6), axis_at), (blocks,), jnp.float32, least / len(shards), high / len(shards))
        level = level * jnp.repeat(jnp.exp(steps), shape[axis_at] // blocks).reshape((-1,) + (1,) * (len(shape) - 1 - axis_at))
    return level


def noise(own_key, dims, scale, reach, shards=(), kind=jnp.bfloat16):
    level = levels(own_key, dims, shards, -0.22, 0.18) if shards else 1.0
    result = jax.random.normal(own_key, dims, jnp.float32) * scale * level
    return jnp.minimum(jnp.maximum(result, -reach), reach).astype(kind)


def setup_inputs(seed: int = 0) -> dict:
    streams_of = jax.random.split(jax.random.key(seed), 7)
    density = noise(streams_of[0], (2, SEGS * C, ANG), 1.0, 6.0, ((1, 32),), jnp.float32)
    near_blocks = noise(streams_of[1], (3, 2, SEGS * C, C), (2 * C) ** -0.5, 0.21875, ((2, 32),))
    projection = noise(streams_of[2], (2, SEGS * R, C), (2 * C) ** -0.5, 0.21875, ((1, 32),))
    transfers = noise(streams_of[3], (LEVELS, 2, SEGS * R, R), (2 * R) ** -0.5, 0.3125, ((2, 32),))
    interpolation = noise(streams_of[4], (2, SEGS * C, R), (2 * R) ** -0.5, 0.3125, ((1, 32),))
    precondition = jnp.clip(0.5 + 1.0 * jax.random.uniform(streams_of[5], (2, SEGS * C), jnp.float32) ** levels(streams_of[5], (2, SEGS * C), ((1, 32),), -0.2, 0.2), 0.5, 1.5)
    return {"density": density, "near_blocks": near_blocks, "projection": projection, "transfers": transfers, "interpolation": interpolation, "precondition": precondition}


def matmul_f32(left, right):
    return jnp.dot(left, right, preferred_element_type=jnp.float32)


def complex_product(matrix, vector):
    real_part = matmul_f32(matrix[0], vector[0]) - matmul_f32(matrix[1], vector[1])
    imag_part = matmul_f32(matrix[0], vector[1]) + matmul_f32(matrix[1], vector[0])
    return jnp.stack([real_part, imag_part])


def paired_product(pair_items):
    return complex_product(pair_items[0], pair_items[1])


def reference(density, near_blocks, projection, transfers, interpolation, precondition):
    dens_low = density.astype(jnp.bfloat16).reshape(2, SEGS, C, ANG)
    before = jnp.moveaxis(jnp.roll(dens_low, 1, axis=1), 1, 0)
    after = jnp.moveaxis(jnp.roll(dens_low, -1, axis=1), 1, 0)
    own_rows = jnp.moveaxis(dens_low, 1, 0)
    near_tiles = jnp.moveaxis(near_blocks.reshape(3, 2, SEGS, C, C), 2, 0)
    proj_tiles = jnp.moveaxis(projection.reshape(2, SEGS, R, C), 1, 0)

    def per_segment(items):
        tiles, mine, prior, later, proj = items
        near_sum = complex_product(tiles[0], mine) + complex_product(tiles[1], prior)
        near_sum = near_sum + complex_product(tiles[2], later)
        return near_sum, complex_product(proj, mine)

    near, coeffs = lax.map(per_segment, (near_tiles, own_rows, before, after, proj_tiles))
    segment_ids = jnp.arange(SEGS, dtype=jnp.int32)
    half_rows = R // 2
    for level_no in range(LEVELS):
        rounded = coeffs.astype(jnp.bfloat16)
        partner = rounded[jnp.bitwise_xor(segment_ids, 2 ** level_no)]
        lower_half = (jnp.bitwise_and(jnp.right_shift(segment_ids, level_no), 1) == 0)[:, None, None, None]
        joined = jnp.where(
            lower_half,
            jnp.concatenate([rounded[:, :, :half_rows], partner[:, :, :half_rows]], axis=2),
            jnp.concatenate([partner[:, :, half_rows:], rounded[:, :, half_rows:]], axis=2),
        )
        level_tiles = jnp.moveaxis(transfers[level_no].reshape(2, SEGS, R, R), 1, 0)
        coeffs = lax.map(paired_product, (level_tiles, joined))
    interp_tiles = jnp.moveaxis(interpolation.reshape(2, SEGS, C, R), 1, 0)
    far = lax.map(paired_product, (interp_tiles, coeffs.astype(jnp.bfloat16)))
    total = jnp.moveaxis(near + far, 0, 1).reshape(2, SEGS * C, ANG)
    pre_real = precondition[0][:, None]
    pre_imag = precondition[1][:, None]
    return jnp.stack([pre_real * total[0] - pre_imag * total[1], pre_real * total[1] + pre_imag * total[0]])
```

```python
import functools

import jax
import jax.numpy as jnp
from jax import lax
from jax.experimental import pallas as pl
from jax.experimental.pallas import tpu as pltpu
from jax.sharding import PartitionSpec as P

MESH = pl.DeviceIdType.MESH
BF16 = jnp.bfloat16
F32 = jnp.float32


def turned(packed):
    width = packed.shape[-1] // 2
    return jnp.concatenate([-packed[:, width:], packed[:, :width]], axis=1)


def packed_product(real, imag, packed):
    return jnp.dot(real, packed, preferred_element_type=F32) + jnp.dot(
        imag, turned(packed), preferred_element_type=F32
    )


def kernel(
    devices,
    levels,
    chunks,
    density_hbm,
    near_hbm,
    projection_hbm,
    transfers_hbm,
    interpolation_hbm,
    total_hbm,
    density,
    near,
    projection,
    transfers,
    interpolation,
    own,
    before,
    after,
    sent,
    joined,
    acc,
    total,
    load_sem,
    out_sem,
    halo_send,
    halo_recv,
    level_send,
    level_recv,
):
    me = lax.axis_index("seg")
    right = lax.rem(me + 1, devices)
    left = lax.rem(me + devices - 1, devices)
    bits = [lax.rem(lax.div(me, 1 << l), 2) for l in range(levels)]
    partners = [me + (1 - 2 * bits[l]) * (1 << l) for l in range(levels)]
    half = projection.shape[1] // 2
    width = density.shape[2] // chunks

    barrier = pltpu.get_barrier_semaphore()
    for other in [left, right] + partners:
        pl.semaphore_signal(barrier, inc=1, device_id=(other,), device_id_type=MESH)

    loads = [
        pltpu.make_async_copy(source, target, load_sem.at[i])
        for i, (source, target) in enumerate(
            [
                (density_hbm, density),
                (projection_hbm, projection),
                (transfers_hbm, transfers),
                (near_hbm, near),
                (interpolation_hbm, interpolation),
            ]
        )
    ]
    for load in loads:
        load.start()

    def to_neighbours(c):
        copies = []
        for way, (other, target) in enumerate([(right, before), (left, after)]):
            copy = pltpu.make_async_remote_copy(
                src_ref=own.at[c],
                dst_ref=target.at[c],
                send_sem=halo_send.at[way, c],
                recv_sem=halo_recv.at[way, c],
                device_id=(other,),
                device_id_type=MESH,
            )
            copy.start()
            copies.append(copy)
        return copies

    def exchange(level, c, coeffs):
        keep = pl.ds(pl.multiple_of(bits[level] * half, half), half)
        give = pl.ds(pl.multiple_of((1 - bits[level]) * half, half), half)
        sent[level, c] = coeffs.astype(BF16)
        copy = pltpu.make_async_remote_copy(
            src_ref=sent.at[level, c, give],
            dst_ref=joined.at[level, c, keep],
            send_sem=level_send.at[level, c],
            recv_sem=level_recv.at[level, c],
            device_id=(partners[level],),
            device_id_type=MESH,
        )
        copy.start()
        joined[level, c, keep] = sent[level, c, keep]
        return copy

    def near_part(block, source, c):
        part = packed_product(near[block, 0], near[block, 1], source[c])
        if block == 0:
            acc[c] = part
        else:
            acc[c] += part

    loads[0].wait()
    for c in range(chunks):
        for part in range(2):
            own[c, :, part * width : (part + 1) * width] = density[
                part, :, c * width : (c + 1) * width
            ].astype(BF16)

    loads[1].wait()
    pl.semaphore_wait(barrier, levels + 2)
    flying = [[None] * chunks for _ in range(levels)]
    halos = [None] * chunks
    for c in range(chunks):
        coeffs = packed_product(projection[0], projection[1], own[c])
        flying[0][c] = exchange(0, c, coeffs)
    for c in range(chunks):
        halos[c] = to_neighbours(c)
    loads[3].wait()
    near_part(0, own, 0)
    loads[2].wait()
    last = [None] * chunks
    for level in range(levels):
        for c in range(chunks):
            flying[level][c].wait_recv()
            coeffs = packed_product(transfers[level, 0], transfers[level, 1], joined[level, c])
            if level + 1 < levels:
                flying[level + 1][c] = exchange(level + 1, c, coeffs)
            else:
                last[c] = coeffs
                if c == 0:
                    loads[4].wait()
                far = packed_product(interpolation[0], interpolation[1], last[c].astype(BF16))
                whole = acc[c] + far
                outs = []
                for part in range(2):
                    columns = slice(c * width, (c + 1) * width)
                    total[part, :, columns] = whole[:, part * width : (part + 1) * width]
                    out = pltpu.make_async_copy(
                        total.at[part, :, pl.ds(c * width, width)],
                        total_hbm.at[part, :, pl.ds(c * width, width)],
                        out_sem.at[c, part],
                    )
                    out.start()
                    outs.append(out)
                last[c] = outs
        if level == 0:
            for c in range(1, chunks):
                near_part(0, own, c)
        if level == 2:
            for c in range(chunks):
                halos[c][0].wait_recv()
                near_part(1, before, c)
        if level == 3:
            for c in range(chunks):
                halos[c][1].wait_recv()
                near_part(2, after, c)
    for c in range(chunks):
        for copy in halos[c] + [flying[level][c] for level in range(levels)]:
            copy.wait_send()
        for out in last[c]:
            out.wait()


def body(density, near_blocks, projection, transfers, interpolation, precondition):
    devices = lax.axis_size("seg")
    levels = transfers.shape[0]
    rows, angles = density.shape[1:]
    rank = projection.shape[1]
    chunks = 2 if angles % 256 == 0 else 1
    packed = 2 * angles // chunks
    any_spec = pl.BlockSpec(memory_space=pl.ANY)
    total = pl.pallas_call(
        functools.partial(kernel, devices, levels, chunks),
        out_shape=jax.ShapeDtypeStruct(density.shape, F32),
        in_specs=[any_spec] * 5,
        out_specs=any_spec,
        scratch_shapes=[
            pltpu.VMEM(density.shape, F32),
            pltpu.VMEM(near_blocks.shape, BF16),
            pltpu.VMEM(projection.shape, BF16),
            pltpu.VMEM(transfers.shape, BF16),
            pltpu.VMEM(interpolation.shape, BF16),
            pltpu.VMEM((chunks, rows, packed), BF16),
            pltpu.VMEM((chunks, rows, packed), BF16),
            pltpu.VMEM((chunks, rows, packed), BF16),
            pltpu.VMEM((levels, chunks, rank, packed), BF16),
            pltpu.VMEM((levels, chunks, rank, packed), BF16),
            pltpu.VMEM((chunks, rows, packed), F32),
            pltpu.VMEM(density.shape, F32),
            pltpu.SemaphoreType.DMA((5,)),
            pltpu.SemaphoreType.DMA((chunks, 2)),
            pltpu.SemaphoreType.DMA((2, chunks)),
            pltpu.SemaphoreType.DMA((2, chunks)),
            pltpu.SemaphoreType.DMA((levels, chunks)),
            pltpu.SemaphoreType.DMA((levels, chunks)),
        ],
        compiler_params=pltpu.CompilerParams(
            collective_id=0, has_side_effects=True, vmem_limit_bytes=48 * 1024 * 1024
        ),
        name="boundary_matvec",
    )(density, near_blocks, projection, transfers, interpolation)
    pre_real = precondition[0][:, None]
    pre_imag = precondition[1][:, None]
    return jnp.stack(
        [pre_real * total[0] - pre_imag * total[1], pre_real * total[1] + pre_imag * total[0]]
    )


def solution(mesh):
    placed = (
        P(None, "seg", None),
        P(None, None, "seg", None),
        P(None, "seg", None),
        P(None, None, "seg", None),
        P(None, "seg", None),
        P(None, "seg"),
    )
    return jax.shard_map(
        body, mesh=mesh, in_specs=placed, out_specs=P(None, "seg", None), check_vma=False
    )
```

```python
import functools

import jax
import jax.numpy as jnp
from jax import lax
from jax.experimental import pallas as pl
from jax.experimental.pallas import tpu as pltpu
from jax.sharding import PartitionSpec as P

MESH = pl.DeviceIdType.MESH
BF16 = jnp.bfloat16
F32 = jnp.float32


def turned(packed):
    width = packed.shape[-1] // 2
    return jnp.concatenate([-packed[:, width:], packed[:, :width]], axis=1)


def packed_product(real, imag, packed):
    return jnp.dot(real, packed, preferred_element_type=F32) + jnp.dot(
        imag, turned(packed), preferred_element_type=F32
    )


def kernel(
    devices,
    levels,
    chunks,
    density_hbm,
    near_hbm,
    projection_hbm,
    transfers_hbm,
    interpolation_hbm,
    precondition_hbm,
    result_hbm,
    density,
    near,
    projection,
    transfers,
    interpolation_turned,
    precondition,
    interpolation,
    scale,
    own,
    chip,
    cross,
    sent,
    joined,
    acc,
    result,
    load_sem,
    out_sem,
    halo_send,
    halo_recv,
    level_send,
    level_recv,
):
    me = lax.axis_index("seg")
    bits = [lax.rem(lax.div(me, 1 << l), 2) for l in range(levels)]
    partners = [me + (1 - 2 * bits[l]) * (1 << l) for l in range(levels)]
    outside = lax.rem(me + devices - 1 + 2 * bits[0], devices)
    neighbours = [partners[0], outside]
    neighbour_blocks = [2 - bits[0], 1 + bits[0]]
    halo = [chip, cross]
    half = projection.shape[1] // 2
    width = density.shape[2] // chunks

    barrier = pltpu.get_barrier_semaphore()
    for other in partners + [outside]:
        pl.semaphore_signal(barrier, inc=1, device_id=(other,), device_id_type=MESH)

    def columns(c):
        return pl.ds(c * width, width)

    density_loads = [
        pltpu.make_async_copy(
            density_hbm.at[:, :, columns(c)], density.at[:, :, columns(c)], load_sem.at[5 + c]
        )
        for c in range(chunks)
    ]
    load_projection, load_transfers, load_near, load_interpolation, load_precondition = [
        pltpu.make_async_copy(source, target, load_sem.at[i])
        for i, (source, target) in enumerate(
            [
                (projection_hbm, projection),
                (transfers_hbm, transfers),
                (near_hbm, near),
                (interpolation_hbm, interpolation_turned),
                (precondition_hbm, precondition),
            ]
        )
    ]
    for load in density_loads:
        load.start()
    load_projection.start()

    def to_neighbour(way, c):
        copy = pltpu.make_async_remote_copy(
            src_ref=own.at[c],
            dst_ref=halo[way].at[c],
            send_sem=halo_send.at[way, c],
            recv_sem=halo_recv.at[way, c],
            device_id=(neighbours[way],),
            device_id_type=MESH,
        )
        copy.start()
        return copy

    def exchange(level, c, coeffs):
        keep = pl.ds(pl.multiple_of(bits[level] * half, half), half)
        give = pl.ds(pl.multiple_of((1 - bits[level]) * half, half), half)
        sent[level, c] = coeffs.astype(BF16)
        copy = pltpu.make_async_remote_copy(
            src_ref=sent.at[level, c, give],
            dst_ref=joined.at[level, c, keep],
            send_sem=level_send.at[level, c],
            recv_sem=level_recv.at[level, c],
            device_id=(partners[level],),
            device_id_type=MESH,
        )
        copy.start()
        joined[level, c, keep] = sent[level, c, keep]
        return copy

    def near_own(c):
        acc[c] = packed_product(near[0, 0], near[0, 1], own[c])

    def near_halo(way, c):
        halos[way][c].wait_recv()
        block = neighbour_blocks[way]
        acc[c] += packed_product(near[block, 0], near[block, 1], halo[way][c])

    halos = [[None] * chunks for _ in range(2)]
    flying = [[None] * chunks for _ in range(levels)]
    for c in range(chunks):
        density_loads[c].wait()
        for part in range(2):
            own[c, :, part * width : (part + 1) * width] = density[
                part, :, c * width : (c + 1) * width
            ].astype(BF16)
        if c == 0:
            pl.semaphore_wait(barrier, levels + 1)
            halos[1][0] = to_neighbour(1, 0)
    load_transfers.start()
    load_near.start()
    load_interpolation.start()
    load_precondition.start()
    load_projection.wait()
    for c in range(chunks):
        flying[0][c] = exchange(0, c, packed_product(projection[0], projection[1], own[c]))
    for c in range(chunks):
        halos[0][c] = to_neighbour(0, c)
    load_near.wait()
    near_own(0)
    load_transfers.wait()

    outs = []
    for level in range(levels):
        for c in range(chunks):
            flying[level][c].wait_recv()
            coeffs = packed_product(transfers[level, 0], transfers[level, 1], joined[level, c])
            if level + 1 < levels:
                flying[level + 1][c] = exchange(level + 1, c, coeffs)
                continue
            far = packed_product(interpolation[0], interpolation[1], coeffs.astype(BF16))
            whole = acc[c] + far
            real, imag = whole[:, :width], whole[:, width:]
            for part, value in enumerate(
                [scale[0] * real - scale[1] * imag, scale[0] * imag + scale[1] * real]
            ):
                result[part, :, c * width : (c + 1) * width] = value
                out = pltpu.make_async_copy(
                    result.at[part, :, columns(c)],
                    result_hbm.at[part, :, columns(c)],
                    out_sem.at[c, part],
                )
                out.start()
                outs.append(out)
        if level == 0:
            for c in range(1, chunks):
                halos[1][c] = to_neighbour(1, c)
            for c in range(1, chunks):
                near_own(c)
        if level == 1:
            for c in range(chunks):
                near_halo(0, c)
        if level == 2:
            load_interpolation.wait()
            load_precondition.wait()
            for part in range(2):
                interpolation[part] = interpolation_turned[part].T
                row = precondition[part : part + 1, :]
                scale[part] = jnp.broadcast_to(row, (width, row.shape[1])).T
        if level == 3:
            for c in range(chunks):
                near_halo(1, c)
    for copies in halos + flying:
        for copy in copies:
            copy.wait_send()
    for out in outs:
        out.wait()


def body(density, near_blocks, projection, transfers, interpolation, precondition):
    devices = lax.axis_size("seg")
    levels = transfers.shape[0]
    rows, angles = density.shape[1:]
    rank = projection.shape[1]
    chunks = 2 if angles % 256 == 0 else 1
    width = angles // chunks
    hbm_spec = pl.BlockSpec(memory_space=pltpu.HBM)
    interpolation_turned = jnp.swapaxes(interpolation, 1, 2)
    return pl.pallas_call(
        functools.partial(kernel, devices, levels, chunks),
        out_shape=jax.ShapeDtypeStruct(density.shape, F32),
        in_specs=[hbm_spec] * 6,
        out_specs=pl.BlockSpec(memory_space=pl.ANY),
        scratch_shapes=[
            pltpu.VMEM(density.shape, F32),
            pltpu.VMEM(near_blocks.shape, BF16),
            pltpu.VMEM(projection.shape, BF16),
            pltpu.VMEM(transfers.shape, BF16),
            pltpu.VMEM(interpolation_turned.shape, BF16),
            pltpu.VMEM(precondition.shape, F32),
            pltpu.VMEM(interpolation.shape, BF16),
            pltpu.VMEM((2, rows, width), F32),
            pltpu.VMEM((chunks, rows, 2 * width), BF16),
            pltpu.VMEM((chunks, rows, 2 * width), BF16),
            pltpu.VMEM((chunks, rows, 2 * width), BF16),
            pltpu.VMEM((levels, chunks, rank, 2 * width), BF16),
            pltpu.VMEM((levels, chunks, rank, 2 * width), BF16),
            pltpu.VMEM((chunks, rows, 2 * width), F32),
            pltpu.VMEM(density.shape, F32),
            pltpu.SemaphoreType.DMA((5 + chunks,)),
            pltpu.SemaphoreType.DMA((chunks, 2)),
            pltpu.SemaphoreType.DMA((2, chunks)),
            pltpu.SemaphoreType.DMA((2, chunks)),
            pltpu.SemaphoreType.DMA((levels, chunks)),
            pltpu.SemaphoreType.DMA((levels, chunks)),
        ],
        compiler_params=pltpu.CompilerParams(
            collective_id=0, has_side_effects=True, vmem_limit_bytes=32 * 1024 * 1024
        ),
        name="boundary_matvec",
    )(
        *[
            pltpu.with_memory_space_constraint(array, pltpu.HBM)
            for array in (
                density,
                near_blocks,
                projection,
                transfers,
                interpolation_turned,
                precondition,
            )
        ]
    )


def solution(mesh):
    placed = (
        P(None, "seg", None),
        P(None, None, "seg", None),
        P(None, "seg", None),
        P(None, None, "seg", None),
        P(None, "seg", None),
        P(None, "seg"),
    )
    return jax.shard_map(
        body, mesh=mesh, in_specs=placed, out_specs=P(None, "seg", None), check_vma=False
    )
```

```python
import functools

import jax
import jax.numpy as jnp
from jax import lax
from jax.experimental import pallas as pl
from jax.experimental.pallas import tpu as pltpu
from jax.sharding import PartitionSpec as P

MESH = pl.DeviceIdType.MESH
BF16 = jnp.bfloat16
F32 = jnp.float32


def turned(packed):
    width = packed.shape[-1] // 2
    return jnp.concatenate([-packed[:, width:], packed[:, :width]], axis=1)


def packed_product(real, imag, packed):
    return jnp.dot(real, packed, preferred_element_type=F32) + jnp.dot(
        imag, turned(packed), preferred_element_type=F32
    )


def kernel(
    devices,
    levels,
    chunks,
    pieces,
    density_hbm,
    near_hbm,
    projection_hbm,
    transfers_hbm,
    interpolation_hbm,
    precondition_hbm,
    result,
    density,
    near,
    projection,
    transfers,
    interpolation_turned,
    precondition,
    interpolation,
    scale,
    own,
    chip,
    cross,
    sent,
    joined,
    acc,
    load_sem,
    halo_send,
    halo_recv,
    level_send,
    level_recv,
):
    me = lax.axis_index("seg")
    bits = [lax.rem(lax.div(me, 1 << l), 2) for l in range(levels)]
    partners = [me + (1 - 2 * bits[l]) * (1 << l) for l in range(levels)]
    outside = lax.rem(me + devices - 1 + 2 * bits[0], devices)
    neighbours = [partners[0], outside]
    neighbour_blocks = [2 - bits[0], 1 + bits[0]]
    halo = [chip, cross]
    half = projection.shape[1] // 2
    width = density.shape[2] // chunks
    piece_rows = density.shape[1] // pieces

    barrier = pltpu.get_barrier_semaphore()
    for other in partners + [outside]:
        pl.semaphore_signal(barrier, inc=1, device_id=(other,), device_id_type=MESH)

    def columns(c):
        return pl.ds(c * width, width)

    density_loads = [
        pltpu.make_async_copy(
            density_hbm.at[:, :, columns(c)], density.at[:, :, columns(c)], load_sem.at[5 + c]
        )
        for c in range(chunks)
    ]
    load_projection, load_transfers, load_near, load_interpolation, load_precondition = [
        pltpu.make_async_copy(source, target, load_sem.at[i])
        for i, (source, target) in enumerate(
            [
                (projection_hbm, projection),
                (transfers_hbm, transfers),
                (near_hbm, near),
                (interpolation_hbm, interpolation_turned),
                (precondition_hbm, precondition),
            ]
        )
    ]
    for load in density_loads:
        load.start()
    load_projection.start()

    def to_neighbour(way, c, piece):
        rows = pl.ds(piece * piece_rows, piece_rows)
        copy = pltpu.make_async_remote_copy(
            src_ref=own.at[c, rows],
            dst_ref=halo[way].at[c, rows],
            send_sem=halo_send.at[way, c, piece],
            recv_sem=halo_recv.at[way, c, piece],
            device_id=(neighbours[way],),
            device_id_type=MESH,
        )
        copy.start()
        halos[way][c].append(copy)

    def exchange(level, c, coeffs):
        keep = pl.ds(pl.multiple_of(bits[level] * half, half), half)
        give = pl.ds(pl.multiple_of((1 - bits[level]) * half, half), half)
        sent[level, c] = coeffs.astype(BF16)
        copy = pltpu.make_async_remote_copy(
            src_ref=sent.at[level, c, give],
            dst_ref=joined.at[level, c, keep],
            send_sem=level_send.at[level, c],
            recv_sem=level_recv.at[level, c],
            device_id=(partners[level],),
            device_id_type=MESH,
        )
        copy.start()
        joined[level, c, keep] = sent[level, c, keep]
        return copy

    def near_own(c):
        acc[c] = packed_product(near[0, 0], near[0, 1], own[c])

    def near_halo(way, c):
        for copy in halos[way][c]:
            copy.wait_recv()
        block = neighbour_blocks[way]
        acc[c] += packed_product(near[block, 0], near[block, 1], halo[way][c])

    halos = [[[] for _ in range(chunks)] for _ in range(2)]
    turns = [(c, piece) for c in range(chunks) for piece in range(pieces)]
    flying = [[None] * chunks for _ in range(levels)]
    for c in range(chunks):
        density_loads[c].wait()
        for part in range(2):
            own[c, :, part * width : (part + 1) * width] = density[
                part, :, c * width : (c + 1) * width
            ].astype(BF16)
        if c == 0:
            pl.semaphore_wait(barrier, levels + 1)
            to_neighbour(1, *turns[0])
    load_transfers.start()
    load_near.start()
    load_interpolation.start()
    load_precondition.start()
    load_projection.wait()
    for c in range(chunks):
        flying[0][c] = exchange(0, c, packed_product(projection[0], projection[1], own[c]))
    for turn in turns:
        to_neighbour(0, *turn)
    load_near.wait()
    near_own(0)
    load_transfers.wait()

    for level in range(levels):
        for c in range(chunks):
            flying[level][c].wait_recv()
            coeffs = packed_product(transfers[level, 0], transfers[level, 1], joined[level, c])
            if level + 1 < levels:
                flying[level + 1][c] = exchange(level + 1, c, coeffs)
                continue
            far = packed_product(interpolation[0], interpolation[1], coeffs.astype(BF16))
            whole = acc[c] + far
            real, imag = whole[:, :width], whole[:, width:]
            for part, value in enumerate(
                [scale[0] * real - scale[1] * imag, scale[0] * imag + scale[1] * real]
            ):
                result[part, :, c * width : (c + 1) * width] = value
        if level + 1 < levels:
            for turn in turns[level + 1 :] if level + 2 == levels else turns[level + 1 : level + 2]:
                to_neighbour(1, *turn)
        if level == 0:
            for c in range(1, chunks):
                near_own(c)
        if level == 1:
            for c in range(chunks):
                near_halo(0, c)
        if level == 2:
            load_interpolation.wait()
            load_precondition.wait()
            for part in range(2):
                interpolation[part] = interpolation_turned[part].T
                row = precondition[part : part + 1, :]
                scale[part] = jnp.broadcast_to(row, (width, row.shape[1])).T
        if level == 3:
            for c in range(chunks):
                near_halo(1, c)
    for copies in halos[0] + halos[1] + flying:
        for copy in copies:
            copy.wait_send()


def body(density, near_blocks, projection, transfers, interpolation, precondition):
    devices = lax.axis_size("seg")
    levels = transfers.shape[0]
    rows, angles = density.shape[1:]
    rank = projection.shape[1]
    chunks = 2 if angles % 256 == 0 else 1
    width = angles // chunks
    pieces = 2 if rows % 32 == 0 else 1
    hbm_spec = pl.BlockSpec(memory_space=pltpu.HBM)
    interpolation_turned = jnp.swapaxes(interpolation, 1, 2)
    return pl.pallas_call(
        functools.partial(kernel, devices, levels, chunks, pieces),
        out_shape=jax.ShapeDtypeStruct(density.shape, F32),
        in_specs=[hbm_spec] * 6,
        out_specs=pl.BlockSpec(memory_space=pltpu.VMEM),
        scratch_shapes=[
            pltpu.VMEM(density.shape, F32),
            pltpu.VMEM(near_blocks.shape, BF16),
            pltpu.VMEM(projection.shape, BF16),
            pltpu.VMEM(transfers.shape, BF16),
            pltpu.VMEM(interpolation_turned.shape, BF16),
            pltpu.VMEM(precondition.shape, F32),
            pltpu.VMEM(interpolation.shape, BF16),
            pltpu.VMEM((2, rows, width), F32),
            pltpu.VMEM((chunks, rows, 2 * width), BF16),
            pltpu.VMEM((chunks, rows, 2 * width), BF16),
            pltpu.VMEM((chunks, rows, 2 * width), BF16),
            pltpu.VMEM((levels, chunks, rank, 2 * width), BF16),
            pltpu.VMEM((levels, chunks, rank, 2 * width), BF16),
            pltpu.VMEM((chunks, rows, 2 * width), F32),
            pltpu.SemaphoreType.DMA((5 + chunks,)),
            pltpu.SemaphoreType.DMA((2, chunks, pieces)),
            pltpu.SemaphoreType.DMA((2, chunks, pieces)),
            pltpu.SemaphoreType.DMA((levels, chunks)),
            pltpu.SemaphoreType.DMA((levels, chunks)),
        ],
        compiler_params=pltpu.CompilerParams(
            collective_id=0, has_side_effects=True, vmem_limit_bytes=32 * 1024 * 1024
        ),
        name="boundary_matvec",
    )(
        *[
            pltpu.with_memory_space_constraint(array, pltpu.HBM)
            for array in (
                density,
                near_blocks,
                projection,
                transfers,
                interpolation_turned,
                precondition,
            )
        ]
    )


def solution(mesh):
    placed = (
        P(None, "seg", None),
        P(None, None, "seg", None),
        P(None, "seg", None),
        P(None, None, "seg", None),
        P(None, "seg", None),
        P(None, "seg"),
    )
    return jax.shard_map(
        body, mesh=mesh, in_specs=placed, out_specs=P(None, "seg", None), check_vma=False
    )
```

```python
import functools

import jax
import jax.numpy as jnp
from jax import lax
from jax.experimental import pallas as pl
from jax.experimental.pallas import tpu as pltpu
from jax.sharding import PartitionSpec as P

MESH = pl.DeviceIdType.MESH
BF16 = jnp.bfloat16
F32 = jnp.float32


def turned(packed):
    width = packed.shape[-1] // 2
    return jnp.concatenate([-packed[:, width:], packed[:, :width]], axis=1)


def packed_product(real, imag, packed):
    return jnp.dot(real, packed, preferred_element_type=F32) + jnp.dot(
        imag, turned(packed), preferred_element_type=F32
    )


def kernel(
    devices,
    levels,
    chunks,
    pieces,
    density_hbm,
    near_hbm,
    projection_hbm,
    transfers_hbm,
    interpolation_hbm,
    precondition_hbm,
    result,
    density,
    near,
    projection,
    transfers,
    interpolation_turned,
    precondition,
    interpolation,
    scale,
    own,
    chip,
    cross,
    sent,
    joined,
    acc,
    load_sem,
    halo_send,
    halo_recv,
    level_send,
    level_recv,
):
    me = lax.axis_index("seg")
    bits = [lax.rem(lax.div(me, 1 << l), 2) for l in range(levels)]
    partners = [me + (1 - 2 * bits[l]) * (1 << l) for l in range(levels)]
    outside = lax.rem(me + devices - 1 + 2 * bits[0], devices)
    neighbours = [partners[0], outside]
    long_route = bits[0] == bits[1]
    neighbour_blocks = [2 - bits[0], 1 + bits[0]]
    halo = [chip, cross]
    half = projection.shape[1] // 2
    width = density.shape[2] // chunks
    piece_rows = density.shape[1] // pieces

    barrier = pltpu.get_barrier_semaphore()
    for other in partners + [outside]:
        pl.semaphore_signal(barrier, inc=1, device_id=(other,), device_id_type=MESH)

    def columns(c):
        return pl.ds(c * width, width)

    density_loads = [
        pltpu.make_async_copy(
            density_hbm.at[:, :, columns(c)], density.at[:, :, columns(c)], load_sem.at[5 + c]
        )
        for c in range(chunks)
    ]
    load_projection, load_transfers, load_near, load_interpolation, load_precondition = [
        pltpu.make_async_copy(source, target, load_sem.at[i])
        for i, (source, target) in enumerate(
            [
                (projection_hbm, projection),
                (transfers_hbm, transfers),
                (near_hbm, near),
                (interpolation_hbm, interpolation_turned),
                (precondition_hbm, precondition),
            ]
        )
    ]
    for load in density_loads:
        load.start()
    load_projection.start()

    def to_neighbour(way, c, piece):
        rows = pl.ds(piece * piece_rows, piece_rows)
        copy = pltpu.make_async_remote_copy(
            src_ref=own.at[c, rows],
            dst_ref=halo[way].at[c, rows],
            send_sem=halo_send.at[way, c, piece],
            recv_sem=halo_recv.at[way, c, piece],
            device_id=(neighbours[way],),
            device_id_type=MESH,
        )
        halos[way][c].append(copy)
        return copy

    def exchange(level, c, coeffs):
        keep = pl.ds(pl.multiple_of(bits[level] * half, half), half)
        give = pl.ds(pl.multiple_of((1 - bits[level]) * half, half), half)
        sent[level, c] = coeffs.astype(BF16)
        copy = pltpu.make_async_remote_copy(
            src_ref=sent.at[level, c, give],
            dst_ref=joined.at[level, c, keep],
            send_sem=level_send.at[level, c],
            recv_sem=level_recv.at[level, c],
            device_id=(partners[level],),
            device_id_type=MESH,
        )
        copy.start()
        joined[level, c, keep] = sent[level, c, keep]
        return copy

    def near_own(c):
        acc[c] = packed_product(near[0, 0], near[0, 1], own[c])

    def near_halo(way, c):
        for copy in halos[way][c]:
            copy.wait_recv()
        block = neighbour_blocks[way]
        acc[c] += packed_product(near[block, 0], near[block, 1], halo[way][c])

    halos = [[[] for _ in range(chunks)] for _ in range(2)]
    turns = [(c, piece) for c in range(chunks) for piece in range(pieces)]
    inner = [to_neighbour(0, *turn) for turn in turns]
    outer = [to_neighbour(1, *turn) for turn in turns]
    split = len(outer) // 2

    def start_outer(first, last):
        if first is not None:
            @pl.when(long_route)
            def _():
                for copy in first:
                    copy.start()
        if last is not None:
            @pl.when(jnp.logical_not(long_route))
            def _():
                for copy in last:
                    copy.start()

    flying = [[None] * chunks for _ in range(levels)]
    for c in range(chunks):
        density_loads[c].wait()
        for part in range(2):
            own[c, :, part * width : (part + 1) * width] = density[
                part, :, c * width : (c + 1) * width
            ].astype(BF16)
    pl.semaphore_wait(barrier, levels + 1)
    start_outer(outer[:split], None)
    load_transfers.start()
    load_near.start()
    load_interpolation.start()
    load_precondition.start()
    load_projection.wait()
    for c in range(chunks):
        flying[0][c] = exchange(0, c, packed_product(projection[0], projection[1], own[c]))
    for copy in inner:
        copy.start()
    load_transfers.wait()

    for level in range(levels):
        for c in range(chunks):
            flying[level][c].wait_recv()
            coeffs = packed_product(transfers[level, 0], transfers[level, 1], joined[level, c])
            if level + 1 < levels:
                flying[level + 1][c] = exchange(level + 1, c, coeffs)
                continue
            far = packed_product(interpolation[0], interpolation[1], coeffs.astype(BF16))
            whole = acc[c] + far
            real, imag = whole[:, :width], whole[:, width:]
            for part, value in enumerate(
                [scale[0] * real - scale[1] * imag, scale[0] * imag + scale[1] * real]
            ):
                result[part, :, c * width : (c + 1) * width] = value
        if level == 0:
            start_outer(outer[split:], outer[:split])
            load_near.wait()
            for c in range(chunks):
                near_own(c)
        if level == 1:
            start_outer(None, outer[split:])
            for c in range(chunks):
                near_halo(0, c)
        if level == 2:
            load_interpolation.wait()
            load_precondition.wait()
            for part in range(2):
                interpolation[part] = interpolation_turned[part].T
                row = precondition[part : part + 1, :]
                scale[part] = jnp.broadcast_to(row, (width, row.shape[1])).T
        if level == 3:
            for c in range(chunks):
                near_halo(1, c)
    for copies in halos[0] + halos[1] + flying:
        for copy in copies:
            copy.wait_send()


def body(density, near_blocks, projection, transfers, interpolation, precondition):
    devices = lax.axis_size("seg")
    levels = transfers.shape[0]
    rows, angles = density.shape[1:]
    rank = projection.shape[1]
    chunks = 2 if angles % 256 == 0 else 1
    width = angles // chunks
    pieces = 2 if rows % 32 == 0 else 1
    hbm_spec = pl.BlockSpec(memory_space=pltpu.HBM)
    interpolation_turned = jnp.swapaxes(interpolation, 1, 2)
    return pl.pallas_call(
        functools.partial(kernel, devices, levels, chunks, pieces),
        out_shape=jax.ShapeDtypeStruct(density.shape, F32),
        in_specs=[hbm_spec] * 6,
        out_specs=pl.BlockSpec(memory_space=pltpu.VMEM),
        scratch_shapes=[
            pltpu.VMEM(density.shape, F32),
            pltpu.VMEM(near_blocks.shape, BF16),
            pltpu.VMEM(projection.shape, BF16),
            pltpu.VMEM(transfers.shape, BF16),
            pltpu.VMEM(interpolation_turned.shape, BF16),
            pltpu.VMEM(precondition.shape, F32),
            pltpu.VMEM(interpolation.shape, BF16),
            pltpu.VMEM((2, rows, width), F32),
            pltpu.VMEM((chunks, rows, 2 * width), BF16),
            pltpu.VMEM((chunks, rows, 2 * width), BF16),
            pltpu.VMEM((chunks, rows, 2 * width), BF16),
            pltpu.VMEM((levels, chunks, rank, 2 * width), BF16),
            pltpu.VMEM((levels, chunks, rank, 2 * width), BF16),
            pltpu.VMEM((chunks, rows, 2 * width), F32),
            pltpu.SemaphoreType.DMA((5 + chunks,)),
            pltpu.SemaphoreType.DMA((2, chunks, pieces)),
            pltpu.SemaphoreType.DMA((2, chunks, pieces)),
            pltpu.SemaphoreType.DMA((levels, chunks)),
            pltpu.SemaphoreType.DMA((levels, chunks)),
        ],
        compiler_params=pltpu.CompilerParams(
            collective_id=0, has_side_effects=True, vmem_limit_bytes=32 * 1024 * 1024
        ),
        name="boundary_matvec",
    )(
        *[
            pltpu.with_memory_space_constraint(array, pltpu.HBM)
            for array in (
                density,
                near_blocks,
                projection,
                transfers,
                interpolation_turned,
                precondition,
            )
        ]
    )


def solution(mesh):
    placed = (
        P(None, "seg", None),
        P(None, None, "seg", None),
        P(None, "seg", None),
        P(None, None, "seg", None),
        P(None, "seg", None),
        P(None, "seg"),
    )
    return jax.shard_map(
        body, mesh=mesh, in_specs=placed, out_specs=P(None, "seg", None), check_vma=False
    )
```

```python
import functools

import jax
import jax.numpy as jnp
from jax import lax
from jax.experimental import pallas as pl
from jax.experimental.pallas import tpu as pltpu
from jax.sharding import PartitionSpec as P

MESH = pl.DeviceIdType.MESH
BF16 = jnp.bfloat16
F32 = jnp.float32


def turned(packed):
    width = packed.shape[-1] // 2
    return jnp.concatenate([-packed[:, width:], packed[:, :width]], axis=1)


def packed_product(real, imag, packed):
    return jnp.dot(real, packed, preferred_element_type=F32) + jnp.dot(
        imag, turned(packed), preferred_element_type=F32
    )


def kernel(
    devices,
    levels,
    chunks,
    pieces,
    density_hbm,
    near_hbm,
    projection_hbm,
    transfers_hbm,
    interpolation_hbm,
    precondition_hbm,
    result,
    density,
    near,
    projection,
    transfers,
    interpolation_turned,
    precondition,
    interpolation,
    scale,
    own,
    chip,
    cross,
    sent,
    joined,
    acc,
    load_sem,
    halo_send,
    halo_recv,
    level_send,
    level_recv,
):
    me = lax.axis_index("seg")
    bits = [lax.rem(lax.div(me, 1 << l), 2) for l in range(levels)]
    partners = [me + (1 - 2 * bits[l]) * (1 << l) for l in range(levels)]
    outside = lax.rem(me + devices - 1 + 2 * bits[0], devices)
    neighbours = [partners[0], outside]
    neighbour_blocks = [2 - bits[0], 1 + bits[0]]
    halo = [chip, cross]
    half = projection.shape[1] // 2
    width = density.shape[2] // chunks
    piece_rows = density.shape[1] // pieces

    barrier = pltpu.get_barrier_semaphore()
    for other in partners + [outside]:
        pl.semaphore_signal(barrier, inc=1, device_id=(other,), device_id_type=MESH)

    def columns(c):
        return pl.ds(c * width, width)

    density_loads = [
        pltpu.make_async_copy(
            density_hbm.at[:, :, columns(c)], density.at[:, :, columns(c)], load_sem.at[5 + c]
        )
        for c in range(chunks)
    ]
    load_projection, load_transfers, load_near, load_interpolation, load_precondition = [
        pltpu.make_async_copy(source, target, load_sem.at[i])
        for i, (source, target) in enumerate(
            [
                (projection_hbm, projection),
                (transfers_hbm, transfers),
                (near_hbm, near),
                (interpolation_hbm, interpolation_turned),
                (precondition_hbm, precondition),
            ]
        )
    ]
    for load in density_loads:
        load.start()
    load_projection.start()

    def to_neighbour(way, c, piece):
        rows = pl.ds(piece * piece_rows, piece_rows)
        copy = pltpu.make_async_remote_copy(
            src_ref=own.at[c, rows],
            dst_ref=halo[way].at[c, rows],
            send_sem=halo_send.at[way, c, piece],
            recv_sem=halo_recv.at[way, c, piece],
            device_id=(neighbours[way],),
            device_id_type=MESH,
        )
        copy.start()
        halos[way][c].append(copy)

    def exchange(level, c, coeffs):
        keep = pl.ds(pl.multiple_of(bits[level] * half, half), half)
        give = pl.ds(pl.multiple_of((1 - bits[level]) * half, half), half)
        sent[level, c] = coeffs.astype(BF16)
        copy = pltpu.make_async_remote_copy(
            src_ref=sent.at[level, c, give],
            dst_ref=joined.at[level, c, keep],
            send_sem=level_send.at[level, c],
            recv_sem=level_recv.at[level, c],
            device_id=(partners[level],),
            device_id_type=MESH,
        )
        copy.start()
        joined[level, c, keep] = sent[level, c, keep]
        return copy

    def near_own(c):
        acc[c] = packed_product(near[0, 0], near[0, 1], own[c])

    def near_halo(way, c):
        for copy in halos[way][c]:
            copy.wait_recv()
        block = neighbour_blocks[way]
        acc[c] += packed_product(near[block, 0], near[block, 1], halo[way][c])

    def finish(c, coeffs):
        far = packed_product(interpolation[0], interpolation[1], coeffs.astype(BF16))
        whole = acc[c] + far
        real, imag = whole[:, :width], whole[:, width:]
        for part, value in enumerate(
            [scale[0] * real - scale[1] * imag, scale[0] * imag + scale[1] * real]
        ):
            result[part, :, c * width : (c + 1) * width] = value

    def prepare_tail():
        load_interpolation.wait()
        load_precondition.wait()
        for part in range(2):
            interpolation[part] = interpolation_turned[part].T
            row = precondition[part : part + 1, :]
            scale[part] = jnp.broadcast_to(row, (width, row.shape[1])).T

    halos = [[[] for _ in range(chunks)] for _ in range(2)]
    turns = [(c, piece) for c in range(chunks) for piece in range(pieces)]
    flying = [[None] * chunks for _ in range(levels)]
    spare = [functools.partial(near_own, c) for c in range(chunks)]
    spare += [functools.partial(near_halo, 0, c) for c in range(chunks)]
    spare.append(prepare_tail)

    def one_spare():
        if spare:
            spare.pop(0)()

    for c in range(chunks):
        density_loads[c].wait()
        for part in range(2):
            own[c, :, part * width : (part + 1) * width] = density[
                part, :, c * width : (c + 1) * width
            ].astype(BF16)
        if c == 0:
            load_transfers.start()
            load_near.start()
            load_interpolation.start()
            load_precondition.start()
            load_projection.wait()
            pl.semaphore_wait(barrier, levels + 1)
        flying[0][c] = exchange(0, c, packed_product(projection[0], projection[1], own[c]))
        if c == 0:
            to_neighbour(1, *turns[0])
    for turn in turns:
        to_neighbour(0, *turn)
    load_transfers.wait()

    for level in range(levels):
        for c in range(chunks):
            flying[level][c].wait_recv()
            coeffs = packed_product(transfers[level, 0], transfers[level, 1], joined[level, c])
            if level + 1 == levels:
                finish(c, coeffs)
                continue
            flying[level + 1][c] = exchange(level + 1, c, coeffs)
            if c == 0:
                if level == 0:
                    load_near.wait()
                one_spare()
        if level + 1 < levels:
            for turn in turns[level + 1 :] if level + 2 == levels else turns[level + 1 : level + 2]:
                to_neighbour(1, *turn)
        if level + 2 == levels:
            while spare:
                one_spare()
            for c in range(chunks):
                near_halo(1, c)
    for copies in halos[0] + halos[1] + flying:
        for copy in copies:
            copy.wait_send()


def body(density, near_blocks, projection, transfers, interpolation, precondition):
    devices = lax.axis_size("seg")
    levels = transfers.shape[0]
    rows, angles = density.shape[1:]
    rank = projection.shape[1]
    chunks = 2 if angles % 256 == 0 else 1
    width = angles // chunks
    pieces = 2 if rows % 32 == 0 else 1
    hbm_spec = pl.BlockSpec(memory_space=pltpu.HBM)
    interpolation_turned = jnp.swapaxes(interpolation, 1, 2)
    return pl.pallas_call(
        functools.partial(kernel, devices, levels, chunks, pieces),
        out_shape=jax.ShapeDtypeStruct(density.shape, F32),
        in_specs=[hbm_spec] * 6,
        out_specs=pl.BlockSpec(memory_space=pltpu.VMEM),
        scratch_shapes=[
            pltpu.VMEM(density.shape, F32),
            pltpu.VMEM(near_blocks.shape, BF16),
            pltpu.VMEM(projection.shape, BF16),
            pltpu.VMEM(transfers.shape, BF16),
            pltpu.VMEM(interpolation_turned.shape, BF16),
            pltpu.VMEM(precondition.shape, F32),
            pltpu.VMEM(interpolation.shape, BF16),
            pltpu.VMEM((2, rows, width), F32),
            pltpu.VMEM((chunks, rows, 2 * width), BF16),
            pltpu.VMEM((chunks, rows, 2 * width), BF16),
            pltpu.VMEM((chunks, rows, 2 * width), BF16),
            pltpu.VMEM((levels, chunks, rank, 2 * width), BF16),
            pltpu.VMEM((levels, chunks, rank, 2 * width), BF16),
            pltpu.VMEM((chunks, rows, 2 * width), F32),
            pltpu.SemaphoreType.DMA((5 + chunks,)),
            pltpu.SemaphoreType.DMA((2, chunks, pieces)),
            pltpu.SemaphoreType.DMA((2, chunks, pieces)),
            pltpu.SemaphoreType.DMA((levels, chunks)),
            pltpu.SemaphoreType.DMA((levels, chunks)),
        ],
        compiler_params=pltpu.CompilerParams(
            collective_id=0, has_side_effects=True, vmem_limit_bytes=32 * 1024 * 1024
        ),
        name="boundary_matvec",
    )(
        *[
            pltpu.with_memory_space_constraint(array, pltpu.HBM)
            for array in (
                density,
                near_blocks,
                projection,
                transfers,
                interpolation_turned,
                precondition,
            )
        ]
    )


def solution(mesh):
    placed = (
        P(None, "seg", None),
        P(None, None, "seg", None),
        P(None, "seg", None),
        P(None, None, "seg", None),
        P(None, "seg", None),
        P(None, "seg"),
    )
    return jax.shard_map(
        body, mesh=mesh, in_specs=placed, out_specs=P(None, "seg", None), check_vma=False
    )
```

```python
import functools

import jax
import jax.numpy as jnp
from jax import lax
from jax.experimental import pallas as pl
from jax.experimental.pallas import tpu as pltpu
from jax.sharding import PartitionSpec as P

MESH = pl.DeviceIdType.MESH
BF16 = jnp.bfloat16
F32 = jnp.float32


def turned(packed):
    width = packed.shape[-1] // 2
    return jnp.concatenate([-packed[:, width:], packed[:, :width]], axis=1)


def packed_product(real, imag, packed):
    return jnp.dot(real, packed, preferred_element_type=F32) + jnp.dot(
        imag, turned(packed), preferred_element_type=F32
    )


def kernel(
    devices,
    levels,
    chunks,
    pieces,
    density_hbm,
    near_hbm,
    projection_hbm,
    transfers_hbm,
    interpolation_hbm,
    precondition_hbm,
    result,
    density,
    near,
    projection,
    transfers,
    interpolation_turned,
    precondition,
    interpolation,
    scale,
    own,
    chip,
    cross,
    sent,
    joined,
    acc,
    load_sem,
    halo_send,
    halo_recv,
    level_send,
    level_recv,
):
    me = lax.axis_index("seg")
    bits = [lax.rem(lax.div(me, 1 << l), 2) for l in range(levels)]
    partners = [me + (1 - 2 * bits[l]) * (1 << l) for l in range(levels)]
    outside = lax.rem(me + devices - 1 + 2 * bits[0], devices)
    neighbours = [partners[0], outside]
    same_plane = bits[1] != bits[2]
    longest = jnp.logical_and(bits[1] == bits[2], bits[0] == bits[1])
    beside = jnp.logical_and(bits[1] == bits[2], bits[0] != bits[1])
    routes = [longest, beside, same_plane]
    neighbour_blocks = [2 - bits[0], 1 + bits[0]]
    halo = [chip, cross]
    half = projection.shape[1] // 2
    width = density.shape[2] // chunks
    piece_rows = density.shape[1] // pieces

    barrier = pltpu.get_barrier_semaphore()
    for other in partners + [outside]:
        pl.semaphore_signal(barrier, inc=1, device_id=(other,), device_id_type=MESH)

    def columns(c):
        return pl.ds(c * width, width)

    density_loads = [
        pltpu.make_async_copy(
            density_hbm.at[:, :, columns(c)], density.at[:, :, columns(c)], load_sem.at[5 + c]
        )
        for c in range(chunks)
    ]
    load_projection, load_transfers, load_near, load_interpolation, load_precondition = [
        pltpu.make_async_copy(source, target, load_sem.at[i])
        for i, (source, target) in enumerate(
            [
                (projection_hbm, projection),
                (transfers_hbm, transfers),
                (near_hbm, near),
                (interpolation_hbm, interpolation_turned),
                (precondition_hbm, precondition),
            ]
        )
    ]
    for load in density_loads:
        load.start()
    load_projection.start()

    def to_neighbour(way, c, piece):
        rows = pl.ds(piece * piece_rows, piece_rows)
        copy = pltpu.make_async_remote_copy(
            src_ref=own.at[c, rows],
            dst_ref=halo[way].at[c, rows],
            send_sem=halo_send.at[way, c, piece],
            recv_sem=halo_recv.at[way, c, piece],
            device_id=(neighbours[way],),
            device_id_type=MESH,
        )
        halos[way][c].append(copy)
        return copy

    def exchange(level, c, coeffs):
        keep = pl.ds(pl.multiple_of(bits[level] * half, half), half)
        give = pl.ds(pl.multiple_of((1 - bits[level]) * half, half), half)
        sent[level, c] = coeffs.astype(BF16)
        copy = pltpu.make_async_remote_copy(
            src_ref=sent.at[level, c, give],
            dst_ref=joined.at[level, c, keep],
            send_sem=level_send.at[level, c],
            recv_sem=level_recv.at[level, c],
            device_id=(partners[level],),
            device_id_type=MESH,
        )
        copy.start()
        joined[level, c, keep] = sent[level, c, keep]
        return copy

    def near_own(c):
        acc[c] = packed_product(near[0, 0], near[0, 1], own[c])

    def near_halo(way, c):
        for copy in halos[way][c]:
            copy.wait_recv()
        block = neighbour_blocks[way]
        acc[c] += packed_product(near[block, 0], near[block, 1], halo[way][c])

    def finish(c, coeffs):
        far = packed_product(interpolation[0], interpolation[1], coeffs.astype(BF16))
        whole = acc[c] + far
        real, imag = whole[:, :width], whole[:, width:]
        for part, value in enumerate(
            [scale[0] * real - scale[1] * imag, scale[0] * imag + scale[1] * real]
        ):
            result[part, :, c * width : (c + 1) * width] = value

    def prepare_tail():
        load_interpolation.wait()
        load_precondition.wait()
        for part in range(2):
            interpolation[part] = interpolation_turned[part].T
            row = precondition[part : part + 1, :]
            scale[part] = jnp.broadcast_to(row, (width, row.shape[1])).T

    halos = [[[] for _ in range(chunks)] for _ in range(2)]
    turns = [(c, piece) for c in range(chunks) for piece in range(pieces)]
    inner = [to_neighbour(0, *turn) for turn in turns]
    outer = [to_neighbour(1, *turn) for turn in turns]

    def start_outer(*runs):
        for route, run in zip(routes, runs):
            if run:
                @pl.when(route)
                def _():
                    for i in run:
                        outer[i].start()

    flying = [[None] * chunks for _ in range(levels)]
    spare = [functools.partial(near_own, c) for c in range(chunks)]
    spare += [functools.partial(near_halo, 0, c) for c in range(chunks)]
    spare.append(prepare_tail)

    def one_spare():
        if spare:
            spare.pop(0)()

    for c in range(chunks):
        density_loads[c].wait()
        for part in range(2):
            own[c, :, part * width : (part + 1) * width] = density[
                part, :, c * width : (c + 1) * width
            ].astype(BF16)
        if c == 0:
            load_transfers.start()
            load_near.start()
            load_interpolation.start()
            load_precondition.start()
            load_projection.wait()
            pl.semaphore_wait(barrier, levels + 1)
        flying[0][c] = exchange(0, c, packed_product(projection[0], projection[1], own[c]))
        if c == 0:
            start_outer([0, 1], [], [0])
    start_outer([2], [], [])
    for copy in inner:
        copy.start()
    load_transfers.wait()

    for level in range(levels):
        for c in range(chunks):
            flying[level][c].wait_recv()
            coeffs = packed_product(transfers[level, 0], transfers[level, 1], joined[level, c])
            if level + 1 == levels:
                finish(c, coeffs)
                continue
            flying[level + 1][c] = exchange(level + 1, c, coeffs)
            if c == 0:
                if level == 0:
                    load_near.wait()
                one_spare()
        if level == 0:
            start_outer([3], [0], [1])
        if level == 1:
            start_outer([], [1, 2], [2])
        if level == 2:
            start_outer([], [3], [3])
        if level + 2 == levels:
            while spare:
                one_spare()
            for c in range(chunks):
                near_halo(1, c)
    for copies in halos[0] + halos[1] + flying:
        for copy in copies:
            copy.wait_send()


def body(density, near_blocks, projection, transfers, interpolation, precondition):
    devices = lax.axis_size("seg")
    levels = transfers.shape[0]
    rows, angles = density.shape[1:]
    rank = projection.shape[1]
    chunks = 2
    width = angles // chunks
    pieces = 2
    hbm_spec = pl.BlockSpec(memory_space=pltpu.HBM)
    interpolation_turned = jnp.swapaxes(interpolation, 1, 2)
    return pl.pallas_call(
        functools.partial(kernel, devices, levels, chunks, pieces),
        out_shape=jax.ShapeDtypeStruct(density.shape, F32),
        in_specs=[hbm_spec] * 6,
        out_specs=pl.BlockSpec(memory_space=pltpu.VMEM),
        scratch_shapes=[
            pltpu.VMEM(density.shape, F32),
            pltpu.VMEM(near_blocks.shape, BF16),
            pltpu.VMEM(projection.shape, BF16),
            pltpu.VMEM(transfers.shape, BF16),
            pltpu.VMEM(interpolation_turned.shape, BF16),
            pltpu.VMEM(precondition.shape, F32),
            pltpu.VMEM(interpolation.shape, BF16),
            pltpu.VMEM((2, rows, width), F32),
            pltpu.VMEM((chunks, rows, 2 * width), BF16),
            pltpu.VMEM((chunks, rows, 2 * width), BF16),
            pltpu.VMEM((chunks, rows, 2 * width), BF16),
            pltpu.VMEM((levels, chunks, rank, 2 * width), BF16),
            pltpu.VMEM((levels, chunks, rank, 2 * width), BF16),
            pltpu.VMEM((chunks, rows, 2 * width), F32),
            pltpu.SemaphoreType.DMA((5 + chunks,)),
            pltpu.SemaphoreType.DMA((2, chunks, pieces)),
            pltpu.SemaphoreType.DMA((2, chunks, pieces)),
            pltpu.SemaphoreType.DMA((levels, chunks)),
            pltpu.SemaphoreType.DMA((levels, chunks)),
        ],
        compiler_params=pltpu.CompilerParams(
            collective_id=0, has_side_effects=True, vmem_limit_bytes=32 * 1024 * 1024
        ),
        name="boundary_matvec",
    )(
        *[
            pltpu.with_memory_space_constraint(array, pltpu.HBM)
            for array in (
                density,
                near_blocks,
                projection,
                transfers,
                interpolation_turned,
                precondition,
            )
        ]
    )


def solution(mesh):
    placed = (
        P(None, "seg", None),
        P(None, None, "seg", None),
        P(None, "seg", None),
        P(None, None, "seg", None),
        P(None, "seg", None),
        P(None, "seg"),
    )
    return jax.shard_map(
        body, mesh=mesh, in_specs=placed, out_specs=P(None, "seg", None), check_vma=False
    )
```

```python
import functools

import jax
import jax.numpy as jnp
from jax import lax
from jax.experimental import pallas as pl
from jax.experimental.pallas import tpu as pltpu
from jax.sharding import PartitionSpec as P

MESH = pl.DeviceIdType.MESH
BF16 = jnp.bfloat16
F32 = jnp.float32


def turned(packed):
    width = packed.shape[-1] // 2
    return jnp.concatenate([-packed[:, width:], packed[:, :width]], axis=1)


def packed_product(real, imag, packed):
    return jnp.dot(real, packed, preferred_element_type=F32) + jnp.dot(
        imag, turned(packed), preferred_element_type=F32
    )


def kernel(
    devices,
    levels,
    chunks,
    pieces,
    density_hbm,
    near_hbm,
    projection_hbm,
    transfers_hbm,
    interpolation_hbm,
    precondition_hbm,
    result,
    density,
    near,
    projection,
    transfers,
    interpolation_turned,
    precondition,
    interpolation,
    scale,
    own,
    chip,
    cross,
    sent,
    joined,
    acc,
    load_sem,
    halo_send,
    halo_recv,
    level_send,
    level_recv,
):
    me = lax.axis_index("seg")
    bits = [lax.rem(lax.div(me, 1 << l), 2) for l in range(levels)]
    partners = [me + (1 - 2 * bits[l]) * (1 << l) for l in range(levels)]
    outside = lax.rem(me + devices - 1 + 2 * bits[0], devices)
    neighbours = [partners[0], outside]
    neighbour_blocks = [2 - bits[0], 1 + bits[0]]
    halo = [chip, cross]
    half = projection.shape[1] // 2
    width = density.shape[2] // chunks
    piece_rows = density.shape[1] // pieces

    barrier = pltpu.get_barrier_semaphore()
    for other in partners + [outside]:
        pl.semaphore_signal(barrier, inc=1, device_id=(other,), device_id_type=MESH)

    def columns(c):
        return pl.ds(c * width, width)

    density_loads = [
        pltpu.make_async_copy(
            density_hbm.at[:, :, columns(c)], density.at[:, :, columns(c)], load_sem.at[5 + c]
        )
        for c in range(chunks)
    ]
    load_projection, load_transfers, load_near, load_interpolation, load_precondition = [
        pltpu.make_async_copy(source, target, load_sem.at[i])
        for i, (source, target) in enumerate(
            [
                (projection_hbm, projection),
                (transfers_hbm, transfers),
                (near_hbm, near),
                (interpolation_hbm, interpolation_turned),
                (precondition_hbm, precondition),
            ]
        )
    ]
    for load in density_loads:
        load.start()
    load_projection.start()

    def to_neighbour(way, c, piece):
        rows = pl.ds(piece * piece_rows, piece_rows)
        copy = pltpu.make_async_remote_copy(
            src_ref=own.at[c, rows],
            dst_ref=halo[way].at[c, rows],
            send_sem=halo_send.at[way, c, piece],
            recv_sem=halo_recv.at[way, c, piece],
            device_id=(neighbours[way],),
            device_id_type=MESH,
        )
        copy.start()
        halos[way][c].append(copy)

    def exchange(level, c, coeffs):
        keep = pl.ds(pl.multiple_of(bits[level] * half, half), half)
        give = pl.ds(pl.multiple_of((1 - bits[level]) * half, half), half)
        sent[level, c] = coeffs.astype(BF16)
        copy = pltpu.make_async_remote_copy(
            src_ref=sent.at[level, c, give],
            dst_ref=joined.at[level, c, keep],
            send_sem=level_send.at[level, c],
            recv_sem=level_recv.at[level, c],
            device_id=(partners[level],),
            device_id_type=MESH,
        )
        copy.start()
        joined[level, c, keep] = sent[level, c, keep]
        return copy

    def near_own(c):
        acc[c] = packed_product(near[0, 0], near[0, 1], own[c])

    def near_halo(way, c):
        for copy in halos[way][c]:
            copy.wait_recv()
        block = neighbour_blocks[way]
        acc[c] += packed_product(near[block, 0], near[block, 1], halo[way][c])

    def finish(c, coeffs):
        far = packed_product(interpolation[0], interpolation[1], coeffs.astype(BF16))
        whole = acc[c] + far
        real, imag = whole[:, :width], whole[:, width:]
        for part, value in enumerate(
            [scale[0] * real - scale[1] * imag, scale[0] * imag + scale[1] * real]
        ):
            result[part, :, c * width : (c + 1) * width] = value

    def prepare_tail():
        load_interpolation.wait()
        load_precondition.wait()
        for part in range(2):
            interpolation[part] = interpolation_turned[part].T
            row = precondition[part : part + 1, :]
            scale[part] = jnp.broadcast_to(row, (width, row.shape[1])).T

    halos = [[[] for _ in range(chunks)] for _ in range(2)]
    turns = [(c, piece) for c in range(chunks) for piece in range(pieces)]
    flying = [[None] * chunks for _ in range(levels)]
    spare = [functools.partial(near_own, c) for c in range(chunks)]
    spare += [functools.partial(near_halo, 0, c) for c in range(chunks)]
    spare.append(prepare_tail)

    def one_spare():
        if spare:
            spare.pop(0)()

    for c in range(chunks):
        density_loads[c].wait()
        for part in range(2):
            own[c, :, part * width : (part + 1) * width] = density[
                part, :, c * width : (c + 1) * width
            ].astype(BF16)
        if c == 0:
            load_transfers.start()
            load_near.start()
            load_interpolation.start()
            load_precondition.start()
            load_projection.wait()
            pl.semaphore_wait(barrier, levels + 1)
        flying[0][c] = exchange(0, c, packed_product(projection[0], projection[1], own[c]))
    load_transfers.wait()

    for level in range(levels):
        for c in range(chunks):
            flying[level][c].wait_recv()
            coeffs = packed_product(transfers[level, 0], transfers[level, 1], joined[level, c])
            if level + 1 == levels:
                finish(c, coeffs)
                continue
            flying[level + 1][c] = exchange(level + 1, c, coeffs)
            if c == 0:
                if level == 0:
                    load_near.wait()
                one_spare()
        if level == 0:
            to_neighbour(1, *turns[0])
            for turn in turns:
                to_neighbour(0, *turn)
        if level + 1 < levels:
            for turn in turns[level + 1 :] if level + 2 == levels else turns[level + 1 : level + 2]:
                to_neighbour(1, *turn)
        if level + 2 == levels:
            while spare:
                one_spare()
            for c in range(chunks):
                near_halo(1, c)
    for copies in halos[0] + halos[1] + flying:
        for copy in copies:
            copy.wait_send()


def body(density, near_blocks, projection, transfers, interpolation, precondition):
    devices = lax.axis_size("seg")
    levels = transfers.shape[0]
    rows, angles = density.shape[1:]
    rank = projection.shape[1]
    chunks = 2 if angles % 256 == 0 else 1
    width = angles // chunks
    pieces = 2 if rows % 32 == 0 else 1
    hbm_spec = pl.BlockSpec(memory_space=pltpu.HBM)
    interpolation_turned = jnp.swapaxes(interpolation, 1, 2)
    return pl.pallas_call(
        functools.partial(kernel, devices, levels, chunks, pieces),
        out_shape=jax.ShapeDtypeStruct(density.shape, F32),
        in_specs=[hbm_spec] * 6,
        out_specs=pl.BlockSpec(memory_space=pltpu.VMEM),
        scratch_shapes=[
            pltpu.VMEM(density.shape, F32),
            pltpu.VMEM(near_blocks.shape, BF16),
            pltpu.VMEM(projection.shape, BF16),
            pltpu.VMEM(transfers.shape, BF16),
            pltpu.VMEM(interpolation_turned.shape, BF16),
            pltpu.VMEM(precondition.shape, F32),
            pltpu.VMEM(interpolation.shape, BF16),
            pltpu.VMEM((2, rows, width), F32),
            pltpu.VMEM((chunks, rows, 2 * width), BF16),
            pltpu.VMEM((chunks, rows, 2 * width), BF16),
            pltpu.VMEM((chunks, rows, 2 * width), BF16),
            pltpu.VMEM((levels, chunks, rank, 2 * width), BF16),
            pltpu.VMEM((levels, chunks, rank, 2 * width), BF16),
            pltpu.VMEM((chunks, rows, 2 * width), F32),
            pltpu.SemaphoreType.DMA((5 + chunks,)),
            pltpu.SemaphoreType.DMA((2, chunks, pieces)),
            pltpu.SemaphoreType.DMA((2, chunks, pieces)),
            pltpu.SemaphoreType.DMA((levels, chunks)),
            pltpu.SemaphoreType.DMA((levels, chunks)),
        ],
        compiler_params=pltpu.CompilerParams(
            collective_id=0, has_side_effects=True, vmem_limit_bytes=32 * 1024 * 1024
        ),
        name="boundary_matvec",
    )(
        *[
            pltpu.with_memory_space_constraint(array, pltpu.HBM)
            for array in (
                density,
                near_blocks,
                projection,
                transfers,
                interpolation_turned,
                precondition,
            )
        ]
    )


def solution(mesh):
    placed = (
        P(None, "seg", None),
        P(None, None, "seg", None),
        P(None, "seg", None),
        P(None, None, "seg", None),
        P(None, "seg", None),
        P(None, "seg"),
    )
    return jax.shard_map(
        body, mesh=mesh, in_specs=placed, out_specs=P(None, "seg", None), check_vma=False
    )
```

```python
import functools

import jax
import jax.numpy as jnp
from jax import lax
from jax.experimental import pallas as pl
from jax.experimental.pallas import tpu as pltpu
from jax.sharding import PartitionSpec as P

MESH = pl.DeviceIdType.MESH
BF16 = jnp.bfloat16
F32 = jnp.float32


def turned(packed):
    width = packed.shape[-1] // 2
    return jnp.concatenate([-packed[:, width:], packed[:, :width]], axis=1)


def packed_product(real, imag, packed):
    return jnp.dot(real, packed, preferred_element_type=F32) + jnp.dot(
        imag, turned(packed), preferred_element_type=F32
    )


def kernel(
    devices,
    levels,
    chunks,
    pieces,
    density_hbm,
    near_hbm,
    projection_hbm,
    transfers_hbm,
    interpolation_hbm,
    precondition_hbm,
    result,
    density,
    near,
    projection,
    transfers,
    interpolation_turned,
    precondition,
    interpolation,
    scale,
    own,
    chip,
    cross,
    sent,
    joined,
    acc,
    load_sem,
    halo_send,
    halo_recv,
    level_send,
    level_recv,
):
    me = lax.axis_index("seg")
    bits = [lax.rem(lax.div(me, 1 << l), 2) for l in range(levels)]
    partners = [me + (1 - 2 * bits[l]) * (1 << l) for l in range(levels)]
    outside = lax.rem(me + devices - 1 + 2 * bits[0], devices)
    neighbours = [partners[0], outside]
    neighbour_blocks = [2 - bits[0], 1 + bits[0]]
    halo = [chip, cross]
    half = projection.shape[1] // 2
    width = density.shape[2] // chunks
    piece_rows = density.shape[1] // pieces

    barrier = pltpu.get_barrier_semaphore()
    for other in partners + [outside]:
        pl.semaphore_signal(barrier, inc=1, device_id=(other,), device_id_type=MESH)

    def columns(c):
        return pl.ds(c * width, width)

    density_loads = [
        pltpu.make_async_copy(
            density_hbm.at[:, :, columns(c)], density.at[:, :, columns(c)], load_sem.at[5 + c]
        )
        for c in range(chunks)
    ]
    load_projection, load_transfers, load_near, load_interpolation, load_precondition = [
        pltpu.make_async_copy(source, target, load_sem.at[i])
        for i, (source, target) in enumerate(
            [
                (projection_hbm, projection),
                (transfers_hbm, transfers),
                (near_hbm, near),
                (interpolation_hbm, interpolation_turned),
                (precondition_hbm, precondition),
            ]
        )
    ]
    for load in density_loads:
        load.start()
    load_projection.start()

    def to_neighbour(way, c, piece):
        rows = pl.ds(piece * piece_rows, piece_rows)
        copy = pltpu.make_async_remote_copy(
            src_ref=own.at[c, rows],
            dst_ref=halo[way].at[c, rows],
            send_sem=halo_send.at[way, c, piece],
            recv_sem=halo_recv.at[way, c, piece],
            device_id=(neighbours[way],),
            device_id_type=MESH,
        )
        copy.start()
        halos[way][c].append(copy)

    def exchange(level, c, coeffs):
        keep = pl.ds(pl.multiple_of(bits[level] * half, half), half)
        give = pl.ds(pl.multiple_of((1 - bits[level]) * half, half), half)
        sent[level, c] = coeffs.astype(BF16)
        copy = pltpu.make_async_remote_copy(
            src_ref=sent.at[level, c, give],
            dst_ref=joined.at[level, c, keep],
            send_sem=level_send.at[level, c],
            recv_sem=level_recv.at[level, c],
            device_id=(partners[level],),
            device_id_type=MESH,
        )
        copy.start()
        joined[level, c, keep] = sent[level, c, keep]
        return copy

    def near_own(c):
        acc[c] = packed_product(near[0, 0], near[0, 1], own[c])

    def near_halo(way, c):
        for copy in halos[way][c]:
            copy.wait_recv()
        block = neighbour_blocks[way]
        acc[c] += packed_product(near[block, 0], near[block, 1], halo[way][c])

    def finish(c, coeffs):
        far = packed_product(interpolation[0], interpolation[1], coeffs.astype(BF16))
        whole = acc[c] + far
        real, imag = whole[:, :width], whole[:, width:]
        for part, value in enumerate(
            [scale[0] * real - scale[1] * imag, scale[0] * imag + scale[1] * real]
        ):
            result[part, :, c * width : (c + 1) * width] = value

    def prepare_tail():
        load_interpolation.wait()
        load_precondition.wait()
        for part in range(2):
            interpolation[part] = interpolation_turned[part].T
            row = precondition[part : part + 1, :]
            scale[part] = jnp.broadcast_to(row, (width, row.shape[1])).T

    halos = [[[] for _ in range(chunks)] for _ in range(2)]
    turns = [(c, piece) for c in range(chunks) for piece in range(pieces)]
    flying = [[None] * chunks for _ in range(levels)]
    spare = [functools.partial(near_own, c) for c in range(chunks)]
    spare += [functools.partial(near_halo, 0, c) for c in range(chunks)]
    spare.append(prepare_tail)

    def one_spare():
        if spare:
            spare.pop(0)()

    for c in range(chunks):
        density_loads[c].wait()
        for part in range(2):
            own[c, :, part * width : (part + 1) * width] = density[
                part, :, c * width : (c + 1) * width
            ].astype(BF16)
        if c == 0:
            load_transfers.start()
            load_near.start()
            load_interpolation.start()
            load_precondition.start()
            load_projection.wait()
            pl.semaphore_wait(barrier, levels + 1)
        flying[0][c] = exchange(0, c, packed_product(projection[0], projection[1], own[c]))
        if c == 0:
            to_neighbour(1, *turns[0])
    for turn in turns:
        to_neighbour(0, *turn)
    load_transfers.wait()

    for level in range(levels):
        for c in range(chunks):
            if level + 1 == levels:
                near_halo(1, c)
            flying[level][c].wait_recv()
            coeffs = packed_product(transfers[level, 0], transfers[level, 1], joined[level, c])
            if level + 1 == levels:
                finish(c, coeffs)
                continue
            flying[level + 1][c] = exchange(level + 1, c, coeffs)
            if c == 0:
                if level == 0:
                    load_near.wait()
                one_spare()
        if level + 1 < levels:
            for turn in turns[level + 1 :] if level + 2 == levels else turns[level + 1 : level + 2]:
                to_neighbour(1, *turn)
        if level + 2 == levels:
            while spare:
                one_spare()
    for copies in halos[0] + halos[1] + flying:
        for copy in copies:
            copy.wait_send()


def body(density, near_blocks, projection, transfers, interpolation, precondition):
    devices = lax.axis_size("seg")
    levels = transfers.shape[0]
    rows, angles = density.shape[1:]
    rank = projection.shape[1]
    chunks = 2 if angles % 256 == 0 else 1
    width = angles // chunks
    pieces = 2 if rows % 32 == 0 else 1
    hbm_spec = pl.BlockSpec(memory_space=pltpu.HBM)
    interpolation_turned = jnp.swapaxes(interpolation, 1, 2)
    return pl.pallas_call(
        functools.partial(kernel, devices, levels, chunks, pieces),
        out_shape=jax.ShapeDtypeStruct(density.shape, F32),
        in_specs=[hbm_spec] * 6,
        out_specs=pl.BlockSpec(memory_space=pltpu.VMEM),
        scratch_shapes=[
            pltpu.VMEM(density.shape, F32),
            pltpu.VMEM(near_blocks.shape, BF16),
            pltpu.VMEM(projection.shape, BF16),
            pltpu.VMEM(transfers.shape, BF16),
            pltpu.VMEM(interpolation_turned.shape, BF16),
            pltpu.VMEM(precondition.shape, F32),
            pltpu.VMEM(interpolation.shape, BF16),
            pltpu.VMEM((2, rows, width), F32),
            pltpu.VMEM((chunks, rows, 2 * width), BF16),
            pltpu.VMEM((chunks, rows, 2 * width), BF16),
            pltpu.VMEM((chunks, rows, 2 * width), BF16),
            pltpu.VMEM((levels, chunks, rank, 2 * width), BF16),
            pltpu.VMEM((levels, chunks, rank, 2 * width), BF16),
            pltpu.VMEM((chunks, rows, 2 * width), F32),
            pltpu.SemaphoreType.DMA((5 + chunks,)),
            pltpu.SemaphoreType.DMA((2, chunks, pieces)),
            pltpu.SemaphoreType.DMA((2, chunks, pieces)),
            pltpu.SemaphoreType.DMA((levels, chunks)),
            pltpu.SemaphoreType.DMA((levels, chunks)),
        ],
        compiler_params=pltpu.CompilerParams(
            collective_id=0, has_side_effects=True, vmem_limit_bytes=32 * 1024 * 1024
        ),
        name="boundary_matvec",
    )(
        *[
            pltpu.with_memory_space_constraint(array, pltpu.HBM)
            for array in (
                density,
                near_blocks,
                projection,
                transfers,
                interpolation_turned,
                precondition,
            )
        ]
    )


def solution(mesh):
    placed = (
        P(None, "seg", None),
        P(None, None, "seg", None),
        P(None, "seg", None),
        P(None, None, "seg", None),
        P(None, "seg", None),
        P(None, "seg"),
    )
    return jax.shard_map(
        body, mesh=mesh, in_specs=placed, out_specs=P(None, "seg", None), check_vma=False
    )
```
